32 devices in a mesh: section: 2 (over x), tensor: 4 (over z), dp: 4 (over y, core).
Axes of the slice: x: 2, y: 2, z: 4, core: 2. Of those that a mesh axis runs over, the one named last changes fastest.
Arguments:
- frames: bfloat16 [8, 128, 768], P('dp'), may hold values from -6 to 6
- cotangent: bfloat16 [8, 128, 768], P('dp'), may hold values from -6 to 6
- gain_one: float32 [2, 768], P('section'), may hold values from 0.25 to 1.75
- shift_one: float32 [2, 768], P('section'), may hold values from -1.5 to 1.5
- w_query: bfloat16 [2, 768, 768], P('section', None, 'tensor'), may hold values from -0.21875 to 0.21875
- query_bias: float32 [2, 768], P('section', 'tensor'), may hold values from -1.5 to 1.5
- w_key: bfloat16 [2, 768, 768], P('section', None, 'tensor'), may hold values from -0.21875 to 0.21875
- w_value: bfloat16 [2, 768, 768], P('section', None, 'tensor'), may hold values from -0.21875 to 0.21875
- value_bias: float32 [2, 768], P('section', 'tensor'), may hold values from -1.5 to 1.5
- w_attn: bfloat16 [2, 768, 768], P('section', 'tensor'), may hold values from -0.875 to 0.875
- attn_bias: float32 [2, 768], P('section'), may hold values from -1.5 to 1.5
- gain_two: float32 [2, 768], P('section'), may hold values from 0.25 to 1.75
- shift_two: float32 [2, 768], P('section'), may hold values from -1.5 to 1.5
- w_inner: bfloat16 [2, 768, 3072], P('section', None, 'tensor'), may hold values from -0.21875 to 0.21875
- inner_bias: float32 [2, 3072], P('section', 'tensor'), may hold values from -1.5 to 1.5
- w_outer: bfloat16 [2, 3072, 768], P('section', 'tensor'), may hold values from -0.109375 to 0.109375
- outer_bias: float32 [2, 768], P('section'), may hold values from -1.5 to 1.5
Outputs:
- layer_outputs: bfloat16 [2, 8, 128, 768], P('section', 'dp')
- layer_input_grads: bfloat16 [2, 8, 128, 768], P('section', 'dp')
- grad_gain_one: float32 [2, 768], P('section', 'dp')
- grad_shift_one: float32 [2, 768], P('section', 'dp')
- grad_w_query: float32 [2, 768, 768], P('section', 'dp', 'tensor')
- grad_query_bias: float32 [2, 768], P('section', ('tensor', 'dp'))
- grad_w_key: float32 [2, 768, 768], P('section', 'dp', 'tensor')
- grad_w_value: float32 [2, 768, 768], P('section', 'dp', 'tensor')
- grad_value_bias: float32 [2, 768], P('section', ('tensor', 'dp'))
- grad_w_attn: float32 [2, 768, 768], P('section', ('tensor', 'dp'))
- grad_attn_bias: float32 [2, 768], P('section', 'dp')
- grad_gain_two: float32 [2, 768], P('section', 'dp')
- grad_shift_two: float32 [2, 768], P('section', 'dp')
- grad_w_inner: float32 [2, 768, 3072], P('section', 'dp', 'tensor')
- grad_inner_bias: float32 [2, 3072], P('section', ('tensor', 'dp'))
- grad_w_outer: float32 [2, 3072, 768], P('section', ('tensor', 'dp'))
- grad_outer_bias: float32 [2, 768], P('section', 'dp')
The draws below stay inside these ranges and needn't reach their ends.
All inputs are finite; a program needn't handle non-finite values.
Results may differ from the reference program's by a relative error of at most 0.025.
Values may be sent and summed in bfloat16 or wider, within the bound.
A program may use at most 128 MiB of HBM per device.

```python
import jax
import jax.numpy as jnp
from jax import lax

D = 768
HEAD_DIM = 64
FF = 3072
SEQ = 128
CLIPS_DEV = 2
CLIPS = 8
LAYERS = 2
N_TENSOR = 4
N_DP = 4


def strengthened(values, stream_key, source, target, blocks, factor):
    def block_of(axis_at):
        return (jnp.arange(values.shape[axis_at]) // (values.shape[axis_at] // blocks)).reshape((-1,) + (1,) * (values.ndim - 1 - axis_at))

    near = jax.random.permutation(stream_key, blocks)[block_of(target)]
    other_side = (block_of(target) + blocks // 2) % blocks
    return jnp.where((block_of(source) == near) | (block_of(source) == other_side), factor * values, values)


def steps_of(rng, dims, cuts, least, high):
    loudness, own = 1.0, jax.random.fold_in(rng, 6)
    for dim, shards_of in cuts:
        steps = jnp.exp(jax.random.uniform(jax.random.fold_in(own, dim), (shards_of,), jnp.float32, least / len(cuts), high / len(cuts)))
        loudness = loudness * jnp.repeat(steps, dims[dim] // shards_of).reshape([-1 if axis == dim else 1 for axis in range(len(dims))])
    return loudness


def gaussian(rng, shape, deviation, limit, pieces=(), held_as=jnp.bfloat16):
    drawn = jax.random.normal(rng, shape, jnp.float32) * deviation
    if len(pieces) > 0:
        drawn = steps_of(rng, shape, pieces, -0.22, 0.18) * drawn
    return jnp.clip(drawn, min=-limit, max=limit).astype(held_as)


def bell_draw_with(rng, dims, scale, most, split, heavy, held_as=jnp.bfloat16):
    array = scale * jax.random.normal(rng, dims, jnp.float32)
    if split:
        array = array * steps_of(rng, dims, split, -0.22, 0.18)
    return jnp.clip(strengthened(array, jax.random.fold_in(rng, 3), *heavy), -most, most).astype(held_as)


def setup_inputs(seed: int = 0) -> dict:
    splits = jax.random.split(jax.random.key(seed), 18)
    frames = gaussian(splits[0], (CLIPS, SEQ, D), 1.0, 6.0, ((0, 4),))
    cotangent = bell_draw_with(splits[1], (CLIPS, SEQ, D), 1.0, 6.0, ((0, 4),), (0, 2, 4, 2.0))
    gain_one = jnp.clip(1.0 + 0.15 * jax.random.normal(splits[2], (LAYERS, D), jnp.float32), 0.25, 1.75)
    shift_one = gaussian(splits[3], (LAYERS, D), 0.3, 1.5, ((0, 2),), jnp.float32)
    w_query = gaussian(splits[4], (LAYERS, D, D), D ** -0.5, 0.21875, ((0, 2), (2, 4)))
    query_bias = gaussian(splits[5], (LAYERS, D), 0.3, 1.5, ((0, 2), (1, 4)), jnp.float32)
    w_key = gaussian(splits[6], (LAYERS, D, D), D ** -0.5, 0.21875, ((0, 2), (2, 4)))
    w_value = gaussian(splits[7], (LAYERS, D, D), D ** -0.5, 0.21875, ((0, 2), (2, 4)))
    value_bias = gaussian(splits[8], (LAYERS, D), 0.3, 1.5, ((0, 2), (1, 4)), jnp.float32)
    w_attn = gaussian(splits[9], (LAYERS, D, D), (D // 16) ** -0.5, 0.875, ((0, 2), (1, 4)))
    attn_bias = gaussian(splits[10], (LAYERS, D), 0.3, 1.5, ((0, 2),), jnp.float32)
    gain_two = jnp.clip(1.0 + 0.15 * jax.random.normal(splits[11], (LAYERS, D), jnp.float32), 0.25, 1.75)
    shift_two = gaussian(splits[12], (LAYERS, D), 0.3, 1.5, ((0, 2),), jnp.float32)
    w_inner = gaussian(splits[13], (LAYERS, D, FF), D ** -0.5, 0.21875, ((0, 2), (2, 4)))
    inner_bias = gaussian(splits[14], (LAYERS, FF), 0.3, 1.5, ((0, 2), (1, 4)), jnp.float32)
    w_outer = gaussian(splits[15], (LAYERS, FF, D), FF ** -0.5, 0.109375, ((0, 2), (1, 4)))
    outer_bias = gaussian(splits[16], (LAYERS, D), 0.3, 1.5, ((0, 2),), jnp.float32)
    return {"frames": frames, "cotangent": cotangent, "gain_one": gain_one, "shift_one": shift_one, "w_query": w_query, "query_bias": query_bias, "w_key": w_key, "w_value": w_value, "value_bias": value_bias, "w_attn": w_attn, "attn_bias": attn_bias, "gain_two": gain_two, "shift_two": shift_two, "w_inner": w_inner, "inner_bias": inner_bias, "w_outer": w_outer, "outer_bias": outer_bias}


@jax.custom_vjp
def low(v):
    return lax.optimization_barrier(v.astype(jnp.bfloat16)).astype(jnp.float32)

@jax.custom_vjp
def low_back(v):
    return v

def low_keep(v):
    return (low(v), None)

def low_pass(kept, grad):
    return (grad,)

def back_keep(v):
    return (v, None)

def back_low(kept, grad):
    return (low(grad),)
low.defvjp(low_keep, low_pass)
low_back.defvjp(back_keep, back_low)
epsilon = 1e-05

def normalize(values, gain, shift):
    center = values - lax.optimization_barrier(jnp.mean(values, axis=-1, keepdims=True))
    spread = lax.optimization_barrier(jnp.mean(center * center, axis=-1, keepdims=True))
    return center * lax.rsqrt(spread + epsilon) * gain + shift

def product(left, right):
    return jnp.einsum('bsd,de->bse', left, right, precision=lax.Precision.HIGHEST)

def encoder_layer(values, weights):
    gain_one, shift_one, w_query, query_bias, w_key, w_value, value_bias, w_attn, attn_bias, gain_two, shift_two, w_inner, inner_bias, w_outer, outer_bias = weights
    batch, length, width = values.shape
    group_width = width // N_TENSOR
    group_hidden = w_inner.shape[1] // N_TENSOR
    heads_each = group_width // HEAD_DIM
    scale = HEAD_DIM ** (-0.5)
    split_shape = (batch, length, heads_each, HEAD_DIM)
    normed = low(normalize(values, gain_one, shift_one))
    attention_terms = []
    for group in range(N_TENSOR):
        columns = slice(group * group_width, (group + 1) * group_width)
        local_in = low_back(normed)
        queries = low(low_back(product(local_in, w_query[:, columns])) + query_bias[columns])
        key_rows = low(low_back(product(local_in, w_key[:, columns])))
        value_rows = low(low_back(product(local_in, w_value[:, columns])) + value_bias[columns])
        scores = low_back(jnp.einsum('bshd,bthd->bhst', queries.reshape(split_shape), key_rows.reshape(split_shape), precision=lax.Precision.HIGHEST) * scale)
        probs = low(jax.nn.softmax(scores, axis=-1))
        mixed = low(low_back(jnp.einsum('bhst,bthd->bshd', probs, value_rows.reshape(split_shape), precision=lax.Precision.HIGHEST)))
        mixed = mixed.reshape(batch, length, group_width)
        attention_terms.append(low(product(mixed, w_attn[columns, :])))
    middle = values + low_back(sum(attention_terms)) + attn_bias
    normed_two = low(normalize(middle, gain_two, shift_two))
    feed_terms = []
    for group in range(N_TENSOR):
        hidden_cols = slice(group * group_hidden, (group + 1) * group_hidden)
        local_two = low_back(normed_two)
        hidden_pre = low_back(product(local_two, w_inner[:, hidden_cols])) + inner_bias[hidden_cols]
        active = low(jax.nn.gelu(hidden_pre, approximate=False))
        feed_terms.append(low(product(active, w_outer[hidden_cols, :])))
    return middle + low_back(sum(feed_terms)) + outer_bias

def reference(frames, cotangent, gain_one, shift_one, w_query, query_bias, w_key, w_value, value_bias, w_attn, attn_bias, gain_two, shift_two, w_inner, inner_bias, w_outer, outer_bias):
    stacked = tuple((weight.astype(jnp.float32) for weight in (gain_one, shift_one, w_query, query_bias, w_key, w_value, value_bias, w_attn, attn_bias, gain_two, shift_two, w_inner, inner_bias, w_outer, outer_bias)))
    layer_zero = tuple((weight[0] for weight in stacked))
    layer_one = tuple((weight[1] for weight in stacked))
    clip_groups = frames.astype(jnp.float32).reshape(N_DP, CLIPS_DEV, SEQ, D)
    grad_groups = cotangent.astype(jnp.float32).reshape(N_DP, CLIPS_DEV, SEQ, D)

    def forward(clips_in, probe_in, first_weights, second_weights):
        boundary = encoder_layer(clips_in, first_weights)
        handed = low_back(low(boundary)) + probe_in
        return (encoder_layer(handed, second_weights), boundary)

    def one_group(totals, pair):
        clips_in, upstream = pair
        probe = jnp.zeros_like(clips_in)
        final, back_fn, boundary = jax.vjp(forward, clips_in, probe, layer_zero, layer_one, has_aux=True)
        clip_grad, probe_grad, grads_zero, grads_one = back_fn(upstream)
        totals = jax.tree.map(jnp.add, totals, (grads_zero, grads_one))
        return (totals, (boundary, final, clip_grad, probe_grad))
    initial = jax.tree.map(jnp.zeros_like, (layer_zero, layer_one))
    totals, (boundaries, finals, clip_grads, probe_grads) = lax.scan(one_group, initial, (clip_groups, grad_groups))
    layer_outputs = jnp.stack([boundaries.reshape(CLIPS, SEQ, D), finals.reshape(CLIPS, SEQ, D)]).astype(jnp.bfloat16)
    layer_input_grads = jnp.stack([clip_grads.reshape(CLIPS, SEQ, D), probe_grads.reshape(CLIPS, SEQ, D)]).astype(jnp.bfloat16)
    grads = [jnp.stack([totals[0][index], totals[1][index]]) for index in range(15)]
    return (layer_outputs, layer_input_grads, grads[0], grads[1], grads[2], grads[3], grads[4], grads[5], grads[6], grads[7], grads[8], grads[9], grads[10], grads[11], grads[12], grads[13], grads[14])
```

```python
import functools

import jax
import jax.numpy as jnp
from jax import lax
from jax.experimental import pallas as pl
from jax.experimental.pallas import tpu as pltpu
from jax.sharding import PartitionSpec as P

HEAD_DIM = 64
EPS = 1e-05
MESH = pl.DeviceIdType.MESH
F32 = jnp.float32
BF16 = jnp.bfloat16


def mm(a, b):
    return lax.dot_general(a, b, (((1,), (0,)), ((), ())), preferred_element_type=F32)


def mm_nt(a, b):
    return lax.dot_general(a, b, (((1,), (1,)), ((), ())), preferred_element_type=F32)


def mm_tn(a, b):
    return lax.dot_general(a, b, (((0,), (0,)), ((), ())), preferred_element_type=F32)


def standard(v):
    center = v - jnp.mean(v, axis=-1, keepdims=True)
    rate = lax.rsqrt(jnp.mean(center * center, axis=-1, keepdims=True) + EPS)
    return center * rate, rate


def norm_back(grad, n, rate, gain):
    e = grad * gain
    return rate * (
        e - jnp.mean(e, axis=-1, keepdims=True) - n * jnp.mean(e * n, axis=-1, keepdims=True)
    )


def column_sum(v):
    return jnp.sum(v, axis=0, keepdims=True)


def kernel(dims, *refs):
    C, S, D, G, F, NT, ND, fused = dims
    R = S // NT
    H = G // HEAD_DIM
    scale = HEAD_DIM**-0.5
    (
        frames, cot, gain1, shift1, w_q, q_b, w_k, w_v, v_b, w_a, a_b,
        gain2, shift2, w_i, i_b, w_o, o_b,
    ) = refs[:17]
    lo_out, lg_out, gi_out, go_out, gx_out, ga_out, sm_out = refs[17:24]
    (
        xbuf, dybuf, wqkv, abuf, qkv, pbuf, obuf, hbuf, cbuf, gpbuf, zbuf,
        part, got, ybuf, dubuf, dhbuf, ghbuf, dqkv, dxbuf,
        gi, go, gx, ga, ri, ro, rx, ra, sm, smr, smd, smdr,
        rs_s, rs_r, ag_s, ag_r, sc_s, sc_r, dp_s, dp_r, se_s, se_r,
    ) = refs[24:]

    sec = lax.axis_index("section")
    me = lax.axis_index("tensor")
    dp = lax.axis_index("dp")

    def peer(o):
        return lax.rem(me + o, NT)

    def dpeer(o):
        return lax.rem(dp + o, ND)

    def clip(c):
        return pl.ds(pl.multiple_of(c * S, S), S)

    def rows(c, t):
        return pl.ds(pl.multiple_of(c * S + t * R, R), R)

    def scatter(ph, c, o):
        return pltpu.make_async_remote_copy(
            src_ref=part.at[ph, rows(c, peer(o))],
            dst_ref=got.at[ph, c, o - 1],
            send_sem=rs_s.at[ph, c, o - 1],
            recv_sem=rs_r.at[ph, c, o - 1],
            device_id={"tensor": peer(o)},
            device_id_type=MESH,
        )

    gathered = (cbuf, ghbuf, ybuf, dxbuf)

    def gather(ph, c, o):
        return pltpu.make_async_remote_copy(
            src_ref=gathered[ph].at[rows(c, me)],
            dst_ref=gathered[ph].at[rows(c, me)],
            send_sem=ag_s.at[ph, c, o - 1],
            recv_sem=ag_r.at[ph, c, o - 1],
            device_id={"tensor": peer(o)},
            device_id_type=MESH,
        )

    def across(ph, c, o):
        src, dst = ((ybuf, xbuf), (dxbuf, dybuf))[ph]
        return pltpu.make_async_remote_copy(
            src_ref=src.at[rows(c, me)],
            dst_ref=dst.at[rows(c, me)],
            send_sem=sc_s.at[ph, c, o],
            recv_sem=sc_r.at[ph, c, o],
            device_id={"section": 1 - sec, "tensor": peer(o)},
            device_id_type=MESH,
        )

    terms = ((gi, ri), (go, ro), (gx, rx), (ga, ra))

    def spread(k, o):
        src, dst = terms[k]
        n = dst.shape[1]
        return pltpu.make_async_remote_copy(
            src_ref=src.at[pl.ds(pl.multiple_of(dpeer(o) * n, n), n)],
            dst_ref=dst.at[o - 1],
            send_sem=dp_s.at[k, o - 1],
            recv_sem=dp_r.at[k, o - 1],
            device_id={"dp": dpeer(o)},
            device_id_type=MESH,
        )

    def small_tensor(o):
        return pltpu.make_async_remote_copy(
            src_ref=sm,
            dst_ref=smr.at[o - 1],
            send_sem=se_s.at[o - 1],
            recv_sem=se_r.at[o - 1],
            device_id={"tensor": peer(o)},
            device_id_type=MESH,
        )

    def small_dp(o):
        return pltpu.make_async_remote_copy(
            src_ref=smd,
            dst_ref=smdr.at[o - 1],
            send_sem=dp_s.at[4, o - 1],
            recv_sem=dp_r.at[4, o - 1],
            device_id={"dp": dpeer(o)},
            device_id_type=MESH,
        )

    def start_all(make, *at):
        for o in range(1, NT):
            make(*at, o).start()

    def land(make, *at):
        for o in range(1, NT):
            make(*at, o).wait_recv()

    def summed(ph, c):
        land(scatter, ph, c)
        total = part[ph, rows(c, me), :].astype(F32)
        for o in range(1, NT):
            total = total + got[ph, c, o - 1].astype(F32)
        return total

    def each(body):
        def step(c, carry):
            body(c)
            return carry

        lax.fori_loop(0, C, step, 0)

    barrier = pltpu.get_barrier_semaphore()
    for o in range(1, NT):
        pl.semaphore_signal(barrier, 1, device_id={"tensor": peer(o)}, device_id_type=MESH)
    for o in range(NT):
        pl.semaphore_signal(
            barrier, 1, device_id={"section": 1 - sec, "tensor": peer(o)}, device_id_type=MESH
        )
    greeted = 2 * NT - 1
    if fused:
        for o in range(1, ND):
            pl.semaphore_signal(barrier, 1, device_id={"dp": dpeer(o)}, device_id_type=MESH)
        greeted += ND - 1

    wqkv[:, 0:G] = w_q[...]
    wqkv[:, G : 2 * G] = w_k[...]
    wqkv[:, 2 * G : 3 * G] = w_v[...]
    sm[...] = jnp.zeros_like(sm)
    smd[...] = jnp.zeros_like(smd)

    @pl.when(sec == 0)
    def _():
        xbuf[...] = frames[...]

    @pl.when(sec == 1)
    def _():
        dybuf[...] = cot[...]

    pl.semaphore_wait(barrier, greeted)

    def attention(c):
        @pl.when(sec == 1)
        def _():
            for o in range(NT):
                across(0, c, o).wait_recv()

        n, _ = standard(xbuf[clip(c), :].astype(F32))
        a = (n * gain1[...] + shift1[...]).astype(BF16)
        abuf[clip(c), :] = a
        pre = mm(a, wqkv[...])
        qkv[clip(c), 0:G] = (pre[:, 0:G] + q_b[...]).astype(BF16)
        qkv[clip(c), G : 2 * G] = pre[:, G : 2 * G].astype(BF16)
        qkv[clip(c), 2 * G : 3 * G] = (pre[:, 2 * G :] + v_b[...]).astype(BF16)
        for h in range(H):
            at = [slice(i * G + h * HEAD_DIM, i * G + (h + 1) * HEAD_DIM) for i in range(3)]
            q, k, v = [qkv[clip(c), s] for s in at]
            s = mm_nt(q, k) * scale
            p = jnp.exp(s - jnp.max(s, axis=-1, keepdims=True))
            p = p / jnp.sum(p, axis=-1, keepdims=True)
            pbuf[c, h] = p
            obuf[clip(c), at[0]] = mm(p.astype(BF16), v).astype(BF16)
        part[0, clip(c), :] = mm(obuf[clip(c), :], w_a[...]).astype(BF16)
        start_all(scatter, 0, c)

    each(attention)

    def middle(c):
        h = xbuf[rows(c, me), :].astype(F32) + summed(0, c) + a_b[...]
        hbuf[c] = h
        n, _ = standard(h)
        cbuf[rows(c, me), :] = (n * gain2[...] + shift2[...]).astype(BF16)
        start_all(gather, 0, c)

    each(middle)

    def feed(c):
        land(gather, 0, c)
        u = mm(cbuf[clip(c), :], w_i[...]) + i_b[...]
        cumulative = 0.5 * (1.0 + lax.erf(u * (0.5**0.5)))
        z = (u * cumulative).astype(BF16)
        zbuf[clip(c), :] = z
        part[1, clip(c), :] = mm(z, w_o[...]).astype(BF16)
        start_all(scatter, 1, c)
        gpbuf[clip(c), :] = cumulative + u * (jnp.exp(-0.5 * u * u) * 0.3989422804014327)

    each(feed)

    def finish(c):
        y = hbuf[c] + summed(1, c) + o_b[...]
        ybuf[rows(c, me), :] = y.astype(BF16)

        @pl.when(sec == 0)
        def _():
            for o in range(NT):
                across(0, c, o).start()

        start_all(gather, 2, c)

    each(finish)

    def feed_back(c):
        @pl.when(sec == 0)
        def _():
            for o in range(NT):
                across(1, c, o).wait_recv()

        gy = dybuf[clip(c), :]
        smd[8:9, :] += column_sum(gy.astype(F32))
        du = mm_nt(gy, w_o[...]) * gpbuf[clip(c), :]
        smd[9:10, 0:F] += column_sum(du)
        du = du.astype(BF16)
        dubuf[clip(c), :] = du
        part[2, clip(c), :] = mm_nt(du, w_i[...]).astype(BF16)
        start_all(scatter, 2, c)

    each(feed_back)

    def weight_grad(out, left, right):
        n = left.shape[1]
        for low in range(0, n, 256):
            high = min(low + 256, n)
            out[low:high, :] = mm_tn(left[:, low:high], right[...]).astype(BF16)

    def send_terms(k):
        if fused:
            for o in range(1, ND):
                spread(k, o).start()

    weight_grad(gi, cbuf, dubuf)
    send_terms(0)
    weight_grad(go, zbuf, dybuf)
    send_terms(1)

    def middle_back(c):
        dc = summed(2, c)
        n, rate = standard(hbuf[c])
        sm[2:3, :] += column_sum(dc * n)
        sm[3:4, :] += column_sum(dc)
        dh = dybuf[rows(c, me), :].astype(F32) + norm_back(dc, n, rate, gain2[...])
        sm[4:5, :] += column_sum(dh)
        dhbuf[c] = dh
        ghbuf[rows(c, me), :] = dh.astype(BF16)
        start_all(gather, 1, c)

    each(middle_back)

    def attention_back(c):
        land(gather, 1, c)
        do = mm_nt(ghbuf[clip(c), :], w_a[...]).astype(BF16)
        for h in range(H):
            at = [slice(i * G + h * HEAD_DIM, i * G + (h + 1) * HEAD_DIM) for i in range(3)]
            q, k, v = [qkv[clip(c), s] for s in at]
            do_h = do[:, at[0]]
            p = pbuf[c, h]
            dv = mm_tn(p.astype(BF16), do_h)
            dp_h = mm_nt(do_h, v)
            ds = (p * (dp_h - jnp.sum(p * dp_h, axis=-1, keepdims=True))).astype(BF16)
            dq = mm(ds, k) * scale
            dk = mm_tn(ds, q) * scale
            smd[10:11, at[0]] += column_sum(dq)
            smd[11:12, at[0]] += column_sum(dv)
            for s, grad in zip(at, (dq, dk, dv)):
                dqkv[clip(c), s] = grad.astype(BF16)
        part[3, clip(c), :] = mm_nt(dqkv[clip(c), :], wqkv[...]).astype(BF16)
        start_all(scatter, 3, c)

    each(attention_back)
    weight_grad(gx, abuf, dqkv)
    send_terms(2)
    weight_grad(ga, obuf, ghbuf)
    send_terms(3)

    def input_back(c):
        da = summed(3, c)
        n, rate = standard(xbuf[rows(c, me), :].astype(F32))
        sm[0:1, :] += column_sum(da * n)
        sm[1:2, :] += column_sum(da)
        dx = dhbuf[c] + norm_back(da, n, rate, gain1[...])
        dxbuf[rows(c, me), :] = dx.astype(BF16)

        @pl.when(sec == 1)
        def _():
            for o in range(NT):
                across(1, c, o).start()

        start_all(gather, 3, c)

    each(input_back)

    start_all(small_tensor)
    land(small_tensor)
    total = sm[...]
    for o in range(1, NT):
        total = total + smr[o - 1]
    smd[0:8, :] = total
    if fused:
        for o in range(1, ND):
            small_dp(o).start()

    each(lambda c: land(gather, 2, c))
    lo_out[...] = ybuf[...]
    each(lambda c: land(gather, 3, c))
    lg_out[...] = dxbuf[...]

    if fused:
        for k, out in enumerate((gi_out, go_out, gx_out, ga_out)):
            src, dst = terms[k]
            n = dst.shape[1]
            total = src[pl.ds(pl.multiple_of(dp * n, n), n), :].astype(F32)
            for o in range(1, ND):
                spread(k, o).wait_recv()
                total = total + dst[o - 1].astype(F32)
            out[...] = total
        total = smd[...]
        for o in range(1, ND):
            small_dp(o).wait_recv()
            total = total + smdr[o - 1]
        sm_out[...] = total
    else:
        gi_out[...] = gi[...]
        go_out[...] = go[...]
        gx_out[...] = gx[...]
        ga_out[...] = ga[...]
        sm_out[...] = smd[...]

    def sent(c):
        for ph in range(4):
            for o in range(1, NT):
                scatter(ph, c, o).wait_send()
                gather(ph, c, o).wait_send()

        @pl.when(sec == 0)
        def _():
            for o in range(NT):
                across(0, c, o).wait_send()

        @pl.when(sec == 1)
        def _():
            for o in range(NT):
                across(1, c, o).wait_send()

    each(sent)
    for o in range(1, NT):
        small_tensor(o).wait_send()
    if fused:
        for o in range(1, ND):
            small_dp(o).wait_send()
            for k in range(4):
                spread(k, o).wait_send()


def local(NT, ND, *args):
    C, S, D = args[0].shape
    G = args[4].shape[2]
    F = args[13].shape[2]
    T = C * S
    R = S // NT
    H = G // HEAD_DIM
    fused = (D // ND) % 16 == 0 and (G // ND) % 16 == 0 and (F // ND) % 16 == 0
    dims = (C, S, D, G, F, NT, ND, fused)
    operands = [v.reshape(T, D) for v in args[:2]]
    operands += [v[0] if v.ndim == 3 else v for v in args[2:]]
    M = ND if fused else 1
    term = F32 if fused else BF16
    shapes = [
        jax.ShapeDtypeStruct((T, D), BF16),
        jax.ShapeDtypeStruct((T, D), BF16),
        jax.ShapeDtypeStruct((D // M, F), term),
        jax.ShapeDtypeStruct((F // M, D), term),
        jax.ShapeDtypeStruct((D // M, 3 * G), term),
        jax.ShapeDtypeStruct((G // M, D), term),
        jax.ShapeDtypeStruct((16, D), F32),
    ]
    peers = max(M - 1, 1)

    def slots(*shape):
        return pltpu.VMEM((peers,) + shape, BF16) if fused else pltpu.VMEM((1, 16, 128), BF16)

    dma = pltpu.SemaphoreType.DMA
    scratch = [
        pltpu.VMEM((T, D), BF16),
        pltpu.VMEM((T, D), BF16),
        pltpu.VMEM((D, 3 * G), BF16),
        pltpu.VMEM((T, D), BF16),
        pltpu.VMEM((T, 3 * G), BF16),
        pltpu.VMEM((C, H, S, S), F32),
        pltpu.VMEM((T, G), BF16),
        pltpu.VMEM((C, R, D), F32),
        pltpu.VMEM((T, D), BF16),
        pltpu.VMEM((T, F), F32),
        pltpu.VMEM((T, F), BF16),
        pltpu.VMEM((4, T, D), BF16),
        pltpu.VMEM((4, C, NT - 1, R, D), BF16),
        pltpu.VMEM((T, D), BF16),
        pltpu.VMEM((T, F), BF16),
        pltpu.VMEM((C, R, D), F32),
        pltpu.VMEM((T, D), BF16),
        pltpu.VMEM((T, 3 * G), BF16),
        pltpu.VMEM((T, D), BF16),
        pltpu.VMEM((D, F), BF16),
        pltpu.VMEM((F, D), BF16),
        pltpu.VMEM((D, 3 * G), BF16),
        pltpu.VMEM((G, D), BF16),
        slots(D // M, F),
        slots(F // M, D),
        slots(D // M, 3 * G),
        slots(G // M, D),
        pltpu.VMEM((8, D), F32),
        pltpu.VMEM((NT - 1, 8, D), F32),
        pltpu.VMEM((16, D), F32),
        pltpu.VMEM((peers, 16, D), F32),
        dma((4, C, NT - 1)),
        dma((4, C, NT - 1)),
        dma((4, C, NT - 1)),
        dma((4, C, NT - 1)),
        dma((2, C, NT)),
        dma((2, C, NT)),
        dma((5, peers)),
        dma((5, peers)),
        dma((NT - 1,)),
        dma((NT - 1,)),
    ]
    spec = pl.BlockSpec(memory_space=pltpu.VMEM)
    lo, lg, gi, go, gx, ga, sm = pl.pallas_call(
        functools.partial(kernel, dims),
        out_shape=shapes,
        in_specs=[spec] * 17,
        out_specs=[spec] * 7,
        scratch_shapes=scratch,
        compiler_params=pltpu.CompilerParams(
            collective_id=0, has_side_effects=True, vmem_limit_bytes=56 * 1024 * 1024
        ),
        cost_estimate=pl.CostEstimate(
            flops=6 * T * D * (4 * G + 2 * F), bytes_accessed=8 * D * F, transcendentals=T * F
        ),
        name="layers",
    )(*operands)
    if not fused:
        gi, go, gx, ga = [
            lax.psum_scatter(v, "dp", scatter_dimension=0, tiled=True).astype(F32)
            for v in (gi, go, gx, ga)
        ]
        sm = lax.psum(sm, "dp")
    at = lax.axis_index("dp")

    def small(row, width):
        n = width // ND
        return lax.dynamic_slice(sm, (row, at * n), (1, n))

    return (
        lo.reshape(1, C, S, D),
        lg.reshape(1, C, S, D),
        small(0, D),
        small(1, D),
        gx[None, :, 0:G],
        small(10, G),
        gx[None, :, G : 2 * G],
        gx[None, :, 2 * G :],
        small(11, G),
        ga[None],
        small(4, D),
        small(2, D),
        small(3, D),
        gi[None],
        small(9, F),
        go[None],
        small(8, D),
    )


def solution(mesh):
    cols = P("section", None, "tensor")
    rows = P("section", "tensor", None)
    wide = P("section", None)
    part = P("section", "tensor")
    clips = P("dp", None, None)
    in_specs = (
        clips, clips, wide, wide, cols, part, cols, cols, part, rows, wide,
        wide, wide, cols, part, rows, wide,
    )
    acts = P("section", "dp", None, None)
    vec = P("section", "dp")
    col_grad = P("section", "dp", "tensor")
    both = P("section", ("tensor", "dp"))
    row_grad = P("section", ("tensor", "dp"), None)
    out_specs = (
        acts, acts, vec, vec, col_grad, both, col_grad, col_grad, both, row_grad, vec,
        vec, vec, col_grad, both, row_grad, vec,
    )
    return jax.shard_map(
        functools.partial(local, mesh.shape["tensor"], mesh.shape["dp"]),
        mesh=mesh,
        in_specs=in_specs,
        out_specs=out_specs,
        check_vma=False,
    )
```

```python
import functools

import jax
import jax.numpy as jnp
from jax import lax
from jax.experimental import pallas as pl
from jax.experimental.pallas import tpu as pltpu
from jax.sharding import PartitionSpec as P

HEAD_DIM = 64
EPS = 1e-05
MESH = pl.DeviceIdType.MESH
F32 = jnp.float32
BF16 = jnp.bfloat16


def mm(a, b):
    return lax.dot_general(a, b, (((1,), (0,)), ((), ())), preferred_element_type=F32)


def mm_nt(a, b):
    return lax.dot_general(a, b, (((1,), (1,)), ((), ())), preferred_element_type=F32)


def mm_tn(a, b):
    return lax.dot_general(a, b, (((0,), (0,)), ((), ())), preferred_element_type=F32)


def standard(v):
    center = v - jnp.mean(v, axis=-1, keepdims=True)
    rate = lax.rsqrt(jnp.mean(center * center, axis=-1, keepdims=True) + EPS)
    return center * rate, rate


def norm_back(grad, n, rate, gain):
    e = grad * gain
    return rate * (
        e - jnp.mean(e, axis=-1, keepdims=True) - n * jnp.mean(e * n, axis=-1, keepdims=True)
    )


def column_sum(v):
    return jnp.sum(v, axis=0, keepdims=True)


def kernel(dims, *refs):
    C, S, D, G, F, NT, ND, fused = dims
    R = S // NT
    H = G // HEAD_DIM
    scale = HEAD_DIM**-0.5
    (
        frames, cot, gain1, shift1, w_q, q_b, w_k, w_v, v_b, w_a, a_b,
        gain2, shift2, w_i, i_b, w_o, o_b,
    ) = refs[:17]
    lo_out, lg_out, gi_out, go_out, gx_out, ga_out, sm_out = refs[17:24]
    (
        xbuf, dybuf, wqkv, abuf, qkv, pbuf, obuf, hbuf, cbuf, gpbuf, zbuf,
        part, got, ybuf, dzbuf, dubuf, dhbuf, ghbuf, dqkv, dxbuf,
        gi, go, gx, ga, ri, ro, rx, ra, sm, smr, smd, smdr,
        wfull, ofull, hfull, wa_s, wa_r, oa_s, oa_r, rs_s, rs_r, ag_s, ag_r, sc_s, sc_r, dp_s, dp_r, se_s, se_r,
    ) = refs[24:]

    sec = lax.axis_index("section")
    me = lax.axis_index("tensor")
    dp = lax.axis_index("dp")

    def peer(o):
        return lax.rem(me + o, NT)

    def dpeer(o):
        return lax.rem(dp + o, ND)

    def clip(c):
        return pl.ds(pl.multiple_of(c * S, S), S)

    def rows(c, t):
        return pl.ds(pl.multiple_of(c * S + t * R, R), R)

    def scatter(ph, c, o):
        return pltpu.make_async_remote_copy(
            src_ref=part.at[ph, rows(c, peer(o))],
            dst_ref=got.at[ph, c, o - 1],
            send_sem=rs_s.at[ph, c, o - 1],
            recv_sem=rs_r.at[ph, c, o - 1],
            device_id={"tensor": peer(o)},
            device_id_type=MESH,
        )

    gathered = (cbuf, ghbuf, ybuf, dxbuf)

    def gather(ph, c, o):
        return pltpu.make_async_remote_copy(
            src_ref=gathered[ph].at[rows(c, me)],
            dst_ref=gathered[ph].at[rows(c, me)],
            send_sem=ag_s.at[ph, c, o - 1],
            recv_sem=ag_r.at[ph, c, o - 1],
            device_id={"tensor": peer(o)},
            device_id_type=MESH,
        )

    def across(ph, c, o):
        src, dst = ((ybuf, xbuf), (dxbuf, dybuf))[ph]
        return pltpu.make_async_remote_copy(
            src_ref=src.at[rows(c, me)],
            dst_ref=dst.at[rows(c, me)],
            send_sem=sc_s.at[ph, c, o],
            recv_sem=sc_r.at[ph, c, o],
            device_id={"section": 1 - sec, "tensor": peer(o)},
            device_id_type=MESH,
        )

    def weight_copy(o):
        return pltpu.make_async_remote_copy(
            src_ref=wfull.at[me],
            dst_ref=wfull.at[me],
            send_sem=wa_s.at[o - 1],
            recv_sem=wa_r.at[o - 1],
            device_id={"tensor": peer(o)},
            device_id_type=MESH,
        )

    def heads_copy(c, o):
        return pltpu.make_async_remote_copy(
            src_ref=ofull.at[me, clip(c)],
            dst_ref=ofull.at[me, clip(c)],
            send_sem=oa_s.at[c, o - 1],
            recv_sem=oa_r.at[c, o - 1],
            device_id={"tensor": peer(o)},
            device_id_type=MESH,
        )

    terms = ((gi, ri), (go, ro), (gx, rx), (ga, ra))

    def spread(k, o):
        src, dst = terms[k]
        n = dst.shape[1]
        return pltpu.make_async_remote_copy(
            src_ref=src.at[pl.ds(pl.multiple_of(dpeer(o) * n, n), n)],
            dst_ref=dst.at[o - 1],
            send_sem=dp_s.at[k, o - 1],
            recv_sem=dp_r.at[k, o - 1],
            device_id={"dp": dpeer(o)},
            device_id_type=MESH,
        )

    def small_tensor(o):
        return pltpu.make_async_remote_copy(
            src_ref=sm,
            dst_ref=smr.at[o - 1],
            send_sem=se_s.at[o - 1],
            recv_sem=se_r.at[o - 1],
            device_id={"tensor": peer(o)},
            device_id_type=MESH,
        )

    def small_dp(o):
        return pltpu.make_async_remote_copy(
            src_ref=smd,
            dst_ref=smdr.at[o - 1],
            send_sem=dp_s.at[4, o - 1],
            recv_sem=dp_r.at[4, o - 1],
            device_id={"dp": dpeer(o)},
            device_id_type=MESH,
        )

    def start_all(make, *at):
        for o in range(1, NT):
            make(*at, o).start()

    def gone(make, *at):
        for o in range(NT):
            make(*at, o).wait_send()

    def land(make, *at):
        for o in range(1, NT):
            make(*at, o).wait_recv()

    def summed(ph, c):
        land(scatter, ph, c)
        total = part[ph, rows(c, me), :].astype(F32)
        for o in range(1, NT):
            total = total + got[ph, c, o - 1].astype(F32)
        return total

    def each(body):
        def step(c, carry):
            body(c)
            return carry

        lax.fori_loop(0, C, step, 0)

    barrier = pltpu.get_barrier_semaphore()
    for o in range(1, NT):
        pl.semaphore_signal(barrier, 1, device_id={"tensor": peer(o)}, device_id_type=MESH)
    for o in range(NT):
        pl.semaphore_signal(
            barrier, 1, device_id={"section": 1 - sec, "tensor": peer(o)}, device_id_type=MESH
        )
    greeted = 2 * NT - 1
    if fused:
        for o in range(1, ND):
            pl.semaphore_signal(barrier, 1, device_id={"dp": dpeer(o)}, device_id_type=MESH)
        greeted += ND - 1

    wqkv[0:G, :] = w_q[...]
    wqkv[G : 2 * G, :] = w_k[...]
    wqkv[2 * G : 3 * G, :] = w_v[...]
    sm[...] = jnp.zeros_like(sm)
    smd[...] = jnp.zeros_like(smd)

    @pl.when(sec == 0)
    def _():
        xbuf[...] = frames[...]

    def outer_back(c):
        gy = dybuf[clip(c), :]
        smd[8:9, :] += column_sum(gy.astype(F32))
        dzbuf[clip(c), :] = mm_nt(gy, w_o[...])

    @pl.when(sec == 1)
    def _():
        dybuf[...] = cot[...]
        each(outer_back)

    pl.semaphore_wait(barrier, greeted)

    @pl.when(sec == 1)
    def _():
        wfull[me] = w_a[...]
        start_all(weight_copy)
        land(weight_copy)

    def attention(c):
        @pl.when(sec == 1)
        def _():
            for o in range(NT):
                across(0, c, o).wait_recv()

        n, _ = standard(xbuf[clip(c), :].astype(F32))
        a = (n * gain1[...] + shift1[...]).astype(BF16)
        abuf[clip(c), :] = a
        pre = mm_nt(a, wqkv[...])
        qkv[clip(c), 0:G] = (pre[:, 0:G] + q_b[...]).astype(BF16)
        qkv[clip(c), G : 2 * G] = pre[:, G : 2 * G].astype(BF16)
        qkv[clip(c), 2 * G : 3 * G] = (pre[:, 2 * G :] + v_b[...]).astype(BF16)
        for h in range(H):
            at = [slice(i * G + h * HEAD_DIM, i * G + (h + 1) * HEAD_DIM) for i in range(3)]
            q, k, v = [qkv[clip(c), s] for s in at]
            s = mm_nt(q, k) * scale
            p = jnp.exp(s - jnp.max(s, axis=-1, keepdims=True))
            p = p / jnp.sum(p, axis=-1, keepdims=True)
            pbuf[c, h] = p
            obuf[clip(c), at[0]] = mm(p.astype(BF16), v).astype(BF16)

        @pl.when(sec == 0)
        def _():
            part[0, clip(c), :] = mm(obuf[clip(c), :], w_a[...]).astype(BF16)
            start_all(scatter, 0, c)

        @pl.when(sec == 1)
        def _():
            ofull[me, clip(c), :] = obuf[clip(c), :]
            start_all(heads_copy, c)

    each(attention)

    def middle(c):
        h = xbuf[rows(c, me), :].astype(F32) + summed(0, c) + a_b[...]
        hbuf[c] = h
        n, _ = standard(h)
        cbuf[rows(c, me), :] = (n * gain2[...] + shift2[...]).astype(BF16)
        start_all(gather, 0, c)

    def middle_whole(c):
        land(heads_copy, c)
        h = xbuf[clip(c), :].astype(F32) + a_b[...]
        for t in range(NT):
            h = h + mm(ofull[t, clip(c), :], wfull[t])
        hfull[...] = h
        hbuf[c] = hfull[pl.ds(pl.multiple_of(me * R, R), R), :]
        n, _ = standard(h)
        cbuf[clip(c), :] = (n * gain2[...] + shift2[...]).astype(BF16)

    @pl.when(sec == 0)
    def _():
        each(middle)

    @pl.when(sec == 1)
    def _():
        each(middle_whole)

    def feed_out(c):
        part[1, clip(c), :] = mm(zbuf[clip(c), :], w_o[...]).astype(BF16)
        start_all(scatter, 1, c)

    def feed(c):
        @pl.when(sec == 0)
        def _():
            land(gather, 0, c)

        u = mm(cbuf[clip(c), :], w_i[...]) + i_b[...]
        cumulative = 0.5 * (1.0 + lax.erf(u * (0.5**0.5)))
        z = (u * cumulative).astype(BF16)
        zbuf[clip(c), :] = z

        @pl.when(sec == 0)
        def _():
            feed_out(c)

        gpbuf[clip(c), :] = cumulative + u * (jnp.exp(-0.5 * u * u) * 0.3989422804014327)

    each(feed)

    def finish(c):
        y = hbuf[c] + summed(1, c) + o_b[...]
        ybuf[rows(c, me), :] = y.astype(BF16)

        @pl.when(sec == 0)
        def _():
            for o in range(NT):
                across(0, c, o).start()

    @pl.when(sec == 0)
    def _():
        each(finish)
        each(lambda c: gone(across, 0, c))
        each(lambda c: start_all(gather, 2, c))

    def feed_back(c):
        @pl.when(sec == 0)
        def _():
            for o in range(NT):
                across(1, c, o).wait_recv()
            outer_back(c)

        du = dzbuf[clip(c), :] * gpbuf[clip(c), :]
        smd[9:10, 0:F] += column_sum(du)
        du = du.astype(BF16)
        dubuf[clip(c), :] = du
        part[2, clip(c), :] = mm_nt(du, w_i[...]).astype(BF16)
        start_all(scatter, 2, c)

    each(feed_back)

    def weight_grad(out, left, right):
        n = left.shape[1]
        for low in range(0, n, 256):
            high = min(low + 256, n)
            out[low:high, :] = mm_tn(left[:, low:high], right[...]).astype(BF16)

    def send_terms(k):
        if fused:
            for o in range(1, ND):
                spread(k, o).start()

    def feed_weights():
        weight_grad(gi, cbuf, dubuf)
        send_terms(0)
        weight_grad(go, zbuf, dybuf)
        send_terms(1)

    def attention_weights():
        weight_grad(gx, abuf, dqkv)
        send_terms(2)
        weight_grad(ga, obuf, ghbuf)
        send_terms(3)

    @pl.when(sec == 0)
    def _():
        feed_weights()

    def middle_back(c):
        dc = summed(2, c)
        n, rate = standard(hbuf[c])
        sm[2:3, :] += column_sum(dc * n)
        sm[3:4, :] += column_sum(dc)
        dh = dybuf[rows(c, me), :].astype(F32) + norm_back(dc, n, rate, gain2[...])
        sm[4:5, :] += column_sum(dh)
        dhbuf[c] = dh
        ghbuf[rows(c, me), :] = dh.astype(BF16)
        start_all(gather, 1, c)

    each(middle_back)

    def attention_back(c):
        land(gather, 1, c)
        do = mm_nt(ghbuf[clip(c), :], w_a[...]).astype(BF16)
        for h in range(H):
            at = [slice(i * G + h * HEAD_DIM, i * G + (h + 1) * HEAD_DIM) for i in range(3)]
            q, k, v = [qkv[clip(c), s] for s in at]
            do_h = do[:, at[0]]
            p = pbuf[c, h]
            dv = mm_tn(p.astype(BF16), do_h)
            dp_h = mm_nt(do_h, v)
            ds = (p * (dp_h - jnp.sum(p * dp_h, axis=-1, keepdims=True))).astype(BF16)
            dq = mm(ds, k) * scale
            dk = mm_tn(ds, q) * scale
            smd[10:11, at[0]] += column_sum(dq)
            smd[11:12, at[0]] += column_sum(dv)
            for s, grad in zip(at, (dq, dk, dv)):
                dqkv[clip(c), s] = grad.astype(BF16)
        part[3, clip(c), :] = mm(dqkv[clip(c), :], wqkv[...]).astype(BF16)
        start_all(scatter, 3, c)

    each(attention_back)

    @pl.when(sec == 0)
    def _():
        attention_weights()

    def input_back(c):
        da = summed(3, c)
        n, rate = standard(xbuf[rows(c, me), :].astype(F32))
        sm[0:1, :] += column_sum(da * n)
        sm[1:2, :] += column_sum(da)
        dx = dhbuf[c] + norm_back(da, n, rate, gain1[...])
        dxbuf[rows(c, me), :] = dx.astype(BF16)

        @pl.when(sec == 1)
        def _():
            for o in range(NT):
                across(1, c, o).start()

    each(input_back)

    @pl.when(sec == 1)
    def _():
        each(lambda c: gone(across, 1, c))
        each(feed_out)
        feed_weights()
        attention_weights()
        each(finish)
        each(lambda c: start_all(gather, 2, c))

    each(lambda c: start_all(gather, 3, c))

    start_all(small_tensor)
    land(small_tensor)
    total = sm[...]
    for o in range(1, NT):
        total = total + smr[o - 1]
    smd[0:8, :] = total
    if fused:
        for o in range(1, ND):
            small_dp(o).start()

    each(lambda c: land(gather, 2, c))
    lo_out[...] = ybuf[...]
    each(lambda c: land(gather, 3, c))
    lg_out[...] = dxbuf[...]

    if fused:
        for k, out in enumerate((gi_out, go_out, gx_out, ga_out)):
            src, dst = terms[k]
            n = dst.shape[1]
            total = src[pl.ds(pl.multiple_of(dp * n, n), n), :].astype(F32)
            for o in range(1, ND):
                spread(k, o).wait_recv()
                total = total + dst[o - 1].astype(F32)
            out[...] = total
        total = smd[...]
        for o in range(1, ND):
            small_dp(o).wait_recv()
            total = total + smdr[o - 1]
        sm_out[...] = total
    else:
        gi_out[...] = gi[...]
        go_out[...] = go[...]
        gx_out[...] = gx[...]
        ga_out[...] = ga[...]
        sm_out[...] = smd[...]

    def sent(c):
        for ph in range(1, 4):
            for o in range(1, NT):
                scatter(ph, c, o).wait_send()
                gather(ph, c, o).wait_send()

        @pl.when(sec == 0)
        def _():
            for o in range(1, NT):
                scatter(0, c, o).wait_send()
                gather(0, c, o).wait_send()

        @pl.when(sec == 1)
        def _():
            for o in range(1, NT):
                heads_copy(c, o).wait_send()

    each(sent)

    @pl.when(sec == 1)
    def _():
        for o in range(1, NT):
            weight_copy(o).wait_send()

    for o in range(1, NT):
        small_tensor(o).wait_send()
    if fused:
        for o in range(1, ND):
            small_dp(o).wait_send()
            for k in range(4):
                spread(k, o).wait_send()


def local(NT, ND, *args):
    C, S, D = args[0].shape
    G = args[4].shape[2]
    F = args[13].shape[2]
    T = C * S
    R = S // NT
    H = G // HEAD_DIM
    fused = (D // ND) % 16 == 0 and (G // ND) % 16 == 0 and (F // ND) % 16 == 0
    dims = (C, S, D, G, F, NT, ND, fused)
    operands = [v.reshape(T, D) for v in args[:2]]
    operands += [v[0] if v.ndim == 3 else v for v in args[2:]]
    for at in (4, 6, 7):
        operands[at] = operands[at].T
    M = ND if fused else 1
    term = F32 if fused else BF16
    shapes = [
        jax.ShapeDtypeStruct((T, D), BF16),
        jax.ShapeDtypeStruct((T, D), BF16),
        jax.ShapeDtypeStruct((D // M, F), term),
        jax.ShapeDtypeStruct((F // M, D), term),
        jax.ShapeDtypeStruct((D // M, 3 * G), term),
        jax.ShapeDtypeStruct((G // M, D), term),
        jax.ShapeDtypeStruct((16, D), F32),
    ]
    peers = max(M - 1, 1)

    def slots(*shape):
        return pltpu.VMEM((peers,) + shape, BF16) if fused else pltpu.VMEM((1, 16, 128), BF16)

    dma = pltpu.SemaphoreType.DMA
    scratch = [
        pltpu.VMEM((T, D), BF16),
        pltpu.VMEM((T, D), BF16),
        pltpu.VMEM((3 * G, D), BF16),
        pltpu.VMEM((T, D), BF16),
        pltpu.VMEM((T, 3 * G), BF16),
        pltpu.VMEM((C, H, S, S), F32),
        pltpu.VMEM((T, G), BF16),
        pltpu.VMEM((C, R, D), F32),
        pltpu.VMEM((T, D), BF16),
        pltpu.VMEM((T, F), F32),
        pltpu.VMEM((T, F), BF16),
        pltpu.VMEM((4, T, D), BF16),
        pltpu.VMEM((4, C, NT - 1, R, D), BF16),
        pltpu.VMEM((T, D), BF16),
        pltpu.VMEM((T, F), F32),
        pltpu.VMEM((T, F), BF16),
        pltpu.VMEM((C, R, D), F32),
        pltpu.VMEM((T, D), BF16),
        pltpu.VMEM((T, 3 * G), BF16),
        pltpu.VMEM((T, D), BF16),
        pltpu.VMEM((D, F), BF16),
        pltpu.VMEM((F, D), BF16),
        pltpu.VMEM((D, 3 * G), BF16),
        pltpu.VMEM((G, D), BF16),
        slots(D // M, F),
        slots(F // M, D),
        slots(D // M, 3 * G),
        slots(G // M, D),
        pltpu.VMEM((8, D), F32),
        pltpu.VMEM((NT - 1, 8, D), F32),
        pltpu.VMEM((16, D), F32),
        pltpu.VMEM((peers, 16, D), F32),
        pltpu.VMEM((NT, G, D), BF16),
        pltpu.VMEM((NT, T, G), BF16),
        pltpu.VMEM((S, D), F32),
        dma((NT - 1,)),
        dma((NT - 1,)),
        dma((C, NT - 1)),
        dma((C, NT - 1)),
        dma((4, C, NT - 1)),
        dma((4, C, NT - 1)),
        dma((4, C, NT - 1)),
        dma((4, C, NT - 1)),
        dma((2, C, NT)),
        dma((2, C, NT)),
        dma((5, peers)),
        dma((5, peers)),
        dma((NT - 1,)),
        dma((NT - 1,)),
    ]
    spec = pl.BlockSpec(memory_space=pltpu.VMEM)
    lo, lg, gi, go, gx, ga, sm = pl.pallas_call(
        functools.partial(kernel, dims),
        out_shape=shapes,
        in_specs=[spec] * 17,
        out_specs=[spec] * 7,
        scratch_shapes=scratch,
        compiler_params=pltpu.CompilerParams(
            collective_id=0, has_side_effects=True, vmem_limit_bytes=56 * 1024 * 1024
        ),
        cost_estimate=pl.CostEstimate(
            flops=6 * T * D * (4 * G + 2 * F), bytes_accessed=8 * D * F, transcendentals=T * F
        ),
        name="layers",
    )(*operands)
    if not fused:
        gi, go, gx, ga = [
            lax.psum_scatter(v, "dp", scatter_dimension=0, tiled=True).astype(F32)
            for v in (gi, go, gx, ga)
        ]
        sm = lax.psum(sm, "dp")
    at = lax.axis_index("dp")

    def small(row, width):
        n = width // ND
        return lax.dynamic_slice(sm, (row, at * n), (1, n))

    return (
        lo.reshape(1, C, S, D),
        lg.reshape(1, C, S, D),
        small(0, D),
        small(1, D),
        gx[None, :, 0:G],
        small(10, G),
        gx[None, :, G : 2 * G],
        gx[None, :, 2 * G :],
        small(11, G),
        ga[None],
        small(4, D),
        small(2, D),
        small(3, D),
        gi[None],
        small(9, F),
        go[None],
        small(8, D),
    )


def solution(mesh):
    cols = P("section", None, "tensor")
    rows = P("section", "tensor", None)
    wide = P("section", None)
    part = P("section", "tensor")
    clips = P("dp", None, None)
    in_specs = (
        clips, clips, wide, wide, cols, part, cols, cols, part, rows, wide,
        wide, wide, cols, part, rows, wide,
    )
    acts = P("section", "dp", None, None)
    vec = P("section", "dp")
    col_grad = P("section", "dp", "tensor")
    both = P("section", ("tensor", "dp"))
    row_grad = P("section", ("tensor", "dp"), None)
    out_specs = (
        acts, acts, vec, vec, col_grad, both, col_grad, col_grad, both, row_grad, vec,
        vec, vec, col_grad, both, row_grad, vec,
    )
    return jax.shard_map(
        functools.partial(local, mesh.shape["tensor"], mesh.shape["dp"]),
        mesh=mesh,
        in_specs=in_specs,
        out_specs=out_specs,
        check_vma=False,
    )
```
